32 devices in a mesh: seq: 16 (over z, y, x), piece: 2 (over core).
Axes of the slice: x: 2, y: 2, z: 4, core: 2. Of those that a mesh axis runs over, the one named last changes fastest.
Arguments:
- query: bfloat16 [2048, 2048], P('seq', 'piece'), may hold values from -64 to 64
- key_rows: bfloat16 [2048, 2048], P('seq', 'piece'), may hold values from -64 to 64
- value_matrix_rows: bfloat16 [2048, 2048], P('seq', 'piece'), may hold values from -6 to 6
- grad_out: bfloat16 [2048, 2048], P('seq', 'piece'), may hold values from -6 to 6
- rel_embed: bfloat16 [512, 64], replicated, may hold values from -6 to 6
Outputs:
- grad_query: bfloat16 [2048, 2048], P('seq', 'piece')
- grad_key: bfloat16 [2048, 2048], P('seq', 'piece')
- grad_value: bfloat16 [2048, 2048], P('seq', 'piece')
- grad_embed: float32 [512, 64], replicated
The draws below stay inside these ranges and needn't reach their ends.
All inputs are finite; a program needn't handle non-finite values.
Results may differ from the reference program's by a relative error of at most 0.0086.
Values may be sent and summed in bfloat16 or wider, within the bound.
A program may use at most 64 MiB of HBM per device.

```python
import jax
import jax.numpy as jnp
from jax import lax

HEADS = 32
HEAD_DIM = 64
BAND_EXTENT = 512
TOK_DEV = 128
WIDTH = 2048
SEQ = 2048


def draw_query(key, part):
    base = jax.random.normal(jax.random.fold_in(key, 1), (SEQ, WIDTH), jnp.float32)
    return jnp.clip(base, -64.0, 64.0).astype(jnp.bfloat16)


def draw_key_rows(key, part):
    base = jax.random.normal(jax.random.fold_in(key, 2), (SEQ, WIDTH), jnp.float32)
    return jnp.clip(base, -64.0, 64.0).astype(jnp.bfloat16)


def block_levels(stream_key, extent, shards, least, largest):
    level, own = 1.0, jax.random.fold_in(stream_key, 6)
    for position, shards_of in shards:
        heights = jnp.exp(jax.random.uniform(jax.random.fold_in(own, position), (shards_of,), jnp.float32, least / len(shards), largest / len(shards)))
        level = level * jnp.repeat(heights, extent[position] // shards_of).reshape([-1 if axis == position else 1 for axis in range(len(extent))])
    return level


def scatter_about(own_key, shape, spread, most, split=(), kind=jnp.bfloat16):
    result = spread * jax.random.normal(own_key, shape, jnp.float32)
    if split:
        result = result * block_levels(own_key, shape, split, -0.22, 0.18)
    return jnp.clip(result, -most, most).astype(kind)


def setup_inputs(seed: int = 0) -> dict:
    key_list = jax.random.split(jax.random.key(seed), 6)
    return {
        "query": draw_query(jax.random.fold_in(key_list[5], 71), 0),
        "key_rows": draw_key_rows(jax.random.fold_in(key_list[5], 71), 0),
        "value_matrix_rows": scatter_about(key_list[2], (SEQ, WIDTH), 1.0, 6.0, ((0, 16), (1, 2))),
        "grad_out": scatter_about(key_list[3], (SEQ, WIDTH), 1.0, 6.0, ((0, 16), (1, 2))),
        "rel_embed": scatter_about(key_list[4], (BAND_EXTENT, HEAD_DIM), 1.0, 6.0),
    }


def skew_rel(along):
    head_count, row_tiles, cols = along.shape
    padded = jnp.pad(along, ((0, 0), (0, 0), (0, row_tiles)))
    flat = padded.reshape(head_count, row_tiles * (cols + row_tiles))[:, :row_tiles * (cols + row_tiles - 1)]
    return flat.reshape(head_count, row_tiles, cols + row_tiles - 1)[:, :, row_tiles:2 * row_tiles]

def unskew_rel(dscore, cols):
    zeros = jnp.zeros(dscore.shape[:2] + (cols,), dscore.dtype)
    _, pull = jax.vjp(skew_rel, zeros)
    return pull(dscore)[0]

def embed_slice(emb_pad, offset, row_tiles):
    return emb_pad[offset + 1:offset + 2 * row_tiles + 1][::-1]

def masked_scores(query, keys, slab, offset, present, scale):
    row_tiles = query.shape[0]
    qf = query.astype(jnp.float32)
    direct = jnp.einsum('thd,shd->hts', qf, keys.astype(jnp.float32))
    along = jnp.einsum('thd,rd->htr', qf, slab.astype(jnp.float32))
    score = scale * (direct + skew_rel(along))
    qpos = lax.broadcasted_iota(jnp.int32, (row_tiles, row_tiles), 0)
    kpos = lax.broadcasted_iota(jnp.int32, (row_tiles, row_tiles), 1)
    dist = offset + qpos - kpos
    valid = (dist >= 0) & (dist < BAND_EXTENT) & present
    return jnp.where(valid[None], score, -jnp.inf)

def pair_grads(prob, query, value_tensor, dout, delta, scale):
    prob_b = prob.astype(jnp.bfloat16)
    dprob = jnp.einsum('thd,shd->hts', dout.astype(jnp.float32), value_tensor.astype(jnp.float32))
    dscore = (prob * (dprob - delta[:, :, None]) * scale).astype(jnp.bfloat16)
    gkey = jnp.einsum('hts,thd->shd', dscore.astype(jnp.float32), query.astype(jnp.float32))
    gvalue = jnp.einsum('hts,thd->shd', prob_b.astype(jnp.float32), dout.astype(jnp.float32))
    return (dscore, gkey, gvalue)

def query_terms(dscore, keys, slab, query):
    dalong = unskew_rel(dscore, slab.shape[0]).astype(jnp.float32)
    dfloat = dscore.astype(jnp.float32)
    gquery = jnp.einsum('hts,shd->thd', dfloat, keys.astype(jnp.float32))
    gquery = gquery + jnp.einsum('htr,rd->thd', dalong, slab.astype(jnp.float32))
    gembed = jnp.einsum('htr,thd->rd', dalong, query.astype(jnp.float32))
    return (gquery, gembed)

def reference(query, key_rows, value_matrix_rows, grad_out, rel_embed):
    sequence_length, width = query.shape
    row_tiles = TOK_DEV
    head_count = HEADS
    head_feature_width = width // head_count
    scale = head_feature_width ** (-0.5)
    reach = BAND_EXTENT // row_tiles
    blocks = sequence_length // row_tiles
    qh = query.reshape(sequence_length, head_count, head_feature_width)
    doh = grad_out.reshape(sequence_length, head_count, head_feature_width)
    kpad = jnp.pad(key_rows.reshape(sequence_length, head_count, head_feature_width), ((BAND_EXTENT, 0), (0, 0), (0, 0)))
    value_padding = jnp.pad(value_matrix_rows.reshape(sequence_length, head_count, head_feature_width), ((BAND_EXTENT, 0), (0, 0), (0, 0)))
    emb_pad = jnp.pad(rel_embed, ((row_tiles, row_tiles + 1), (0, 0)))
    slabs = [embed_slice(emb_pad, step * row_tiles, row_tiles) for step in range(reach + 1)]

    def block_step(carry, index):
        gk_acc, gv_acc, ge_acc = carry
        start = (index * row_tiles).astype(jnp.int32)
        qb = lax.dynamic_slice_in_dim(qh, start, row_tiles, 0)
        dob = lax.dynamic_slice_in_dim(doh, start, row_tiles, 0)
        keys = []
        value_tensor = []
        scores = []
        for step in range(reach + 1):
            key_begin_index = (start - step * row_tiles + BAND_EXTENT).astype(jnp.int32)
            keys.append(lax.dynamic_slice_in_dim(kpad, key_begin_index, row_tiles, 0))
            value_tensor.append(lax.dynamic_slice_in_dim(value_padding, key_begin_index, row_tiles, 0))
            scores.append(masked_scores(qb, keys[step], slabs[step], step * row_tiles, index >= step, scale))
        top = scores[0].max(axis=2)
        for score in scores[1:]:
            top = jnp.maximum(top, score.max(axis=2))
        total = jnp.zeros_like(top)
        for score in scores:
            total = total + jnp.exp(score - top[:, :, None]).sum(axis=2)
        lse = top + jnp.log(total)
        probs = [jnp.exp(score - lse[:, :, None]) for score in scores]
        attn_out = jnp.zeros((row_tiles, head_count, head_feature_width), jnp.float32)
        for step in range(reach + 1):
            attn_out = attn_out + jnp.einsum('hts,shd->thd', probs[step].astype(jnp.bfloat16).astype(jnp.float32), value_tensor[step].astype(jnp.float32))
        delta = lax.optimization_barrier(jnp.sum(dob.astype(jnp.float32) * attn_out, axis=2)).T
        grad_q = jnp.zeros((row_tiles, head_count, head_feature_width), jnp.float32)
        for step in range(reach + 1):
            dscore, gkey, gvalue = pair_grads(probs[step], qb, value_tensor[step], dob, delta, scale)
            gquery, gembed = query_terms(dscore, keys[step], slabs[step], qb)
            grad_q = grad_q + gquery
            offset = step * row_tiles
            ge_acc = ge_acc.at[offset + 1:offset + 2 * row_tiles + 1].add(gembed[::-1])
            key_begin_index = (start - step * row_tiles + BAND_EXTENT).astype(jnp.int32)
            old_k = lax.dynamic_slice_in_dim(gk_acc, key_begin_index, row_tiles, 0)
            gk_acc = lax.dynamic_update_slice_in_dim(gk_acc, old_k + gkey, key_begin_index, 0)
            old_v = lax.dynamic_slice_in_dim(gv_acc, key_begin_index, row_tiles, 0)
            gv_acc = lax.dynamic_update_slice_in_dim(gv_acc, old_v + gvalue, key_begin_index, 0)
        return ((gk_acc, gv_acc, ge_acc), grad_q.astype(jnp.bfloat16))
    init = (jnp.zeros((sequence_length + BAND_EXTENT, head_count, head_feature_width), jnp.float32), jnp.zeros((sequence_length + BAND_EXTENT, head_count, head_feature_width), jnp.float32), jnp.zeros(emb_pad.shape, jnp.float32))
    (gk_acc, gv_acc, ge_acc), grad_q = lax.scan(block_step, init, jnp.arange(blocks, dtype=jnp.int32))
    grad_query = grad_q.reshape(sequence_length, width)
    grad_key = gk_acc[BAND_EXTENT:].reshape(sequence_length, width).astype(jnp.bfloat16)
    grad_value = gv_acc[BAND_EXTENT:].reshape(sequence_length, width).astype(jnp.bfloat16)
    return (grad_query, grad_key, grad_value, ge_acc[row_tiles:row_tiles + BAND_EXTENT])
```

```python
import functools

import jax
import jax.numpy as jnp
from jax import lax
from jax.experimental import pallas as pl
from jax.experimental.pallas import tpu as pltpu
from jax.sharding import PartitionSpec as P

HEAD_DIM = 64
BAND_EXTENT = 512
LANES = 128
MESH = pl.DeviceIdType.MESH
NT = (((1,), (1,)), ((), ()))
NEG = float("-inf")


def dot(left, right, dims=(((1,), (0,)), ((), ()))):
    return lax.dot_general(left, right, dims, preferred_element_type=jnp.float32)


def skew(along):
    return pltpu.roll(along, 1, 1, stride=1, stride_axis=0)


def mirror(size):
    down = lax.broadcasted_iota(jnp.int32, (size, size), 0)
    across = lax.broadcasted_iota(jnp.int32, (size, size), 1)
    return (down + across == size - 1).astype(jnp.float32).astype(jnp.bfloat16)


def reverse_columns(value, flips):
    parts, stop = [], value.shape[1]
    wide = flips.shape[0]
    while stop:
        size = stop % wide or wide
        parts.append(dot(value[:, stop - size : stop], flips[wide - size :, :size]))
        stop -= size
    return jnp.concatenate(parts, axis=1)


def band_kernel(
    seq_count, piece_count, group, pairs,
    q_ref, k_ref, v_ref, do_ref, emb_ref,
    gq_ref, gk_ref, gv_ref, ge_ref,
    qg, dg, kg, vg, ql, kl, vl, sq, sk, sv, dkt, dvt, det, ee, en,
    de_own, l1, s2, l2, s3, de_all,
    in_s, in_r, h_s, h_r, q_s, q_r, own_s, own_r, back_s, back_r, e1_s, e1_r, e2_s, e2_r, e3_s, e3_r,
):
    rows = q_ref.shape[0]
    band = group * rows
    window = band + rows
    groups = seq_count // group
    mates = group * piece_count
    feat = HEAD_DIM // mates
    seq, piece = lax.axis_index("seq"), lax.axis_index("piece")
    mine, member = seq // group, seq % group
    place = member * piece_count + piece
    has_prev, has_next = mine > 0, mine < groups - 1

    def at(which, index, core):
        return (which * group + index, core)

    def mate(step):
        other = lax.rem(place + step, mates)
        return other, at(mine, other // piece_count, lax.rem(other, piece_count))

    barrier = pltpu.get_barrier_semaphore()

    def greet(device):
        pl.semaphore_signal(barrier, inc=1, device_id=device, device_id_type=MESH)

    for step in range(1, mates):
        greet(mate(step)[1])
    for step in range(1, groups):
        greet(at(lax.rem(mine + step, groups), member, piece))

    @pl.when(has_prev)
    def _():
        for step in range(1, group):
            greet(at(mine - 1, lax.rem(member + step, group), piece))

    @pl.when(has_next)
    def _():
        for step in range(1, group):
            greet(at(mine + 1, lax.rem(member + step, group), piece))

    sides = jnp.where(has_prev, 1, 0) + jnp.where(has_next, 1, 0)
    pl.semaphore_wait(barrier, mates - 1 + groups - 1 + (group - 1) * sides)

    def cols(owner, pair):
        return pl.ds(pl.multiple_of((owner * pairs + pair) * LANES, LANES), LANES)

    def block(index):
        return pl.ds(pl.multiple_of(index * rows, rows), rows)

    def spread(kind, pair, step):
        source = (k_ref, v_ref, q_ref, do_ref)[kind]
        target = (kg, vg, qg, dg)[kind]
        base = (group, group, 0, 0)[kind]
        to = lax.rem(member + step, group)
        return pltpu.make_async_remote_copy(
            src_ref=source.at[:, cols(to, pair)],
            dst_ref=target.at[pair, block(base + member)],
            send_sem=in_s.at[kind, pair, step], recv_sem=in_r.at[kind, pair, step],
            device_id=at(mine, to, piece), device_id_type=MESH,
        )

    def forward(kind, pair, index):
        target = (kg, vg)[kind]
        return pltpu.make_async_remote_copy(
            src_ref=target.at[pair, block(group + index)],
            dst_ref=target.at[pair, block(index)],
            send_sem=h_s.at[kind, pair, index], recv_sem=h_r.at[kind, pair, index],
            device_id=at(mine + 1, member, piece), device_id_type=MESH,
        )

    def to_query_owner(pair, index):
        return pltpu.make_async_remote_copy(
            src_ref=sq.at[pair, index], dst_ref=ql.at[member, pair],
            send_sem=q_s.at[pair, index], recv_sem=q_r.at[pair, member],
            device_id=at(mine, index, piece), device_id_type=MESH,
        )

    def to_key_owner(kind, pair, index):
        return pltpu.make_async_remote_copy(
            src_ref=(sk, sv)[kind].at[pair, group + index], dst_ref=(kl, vl)[kind].at[0, member, pair],
            send_sem=own_s.at[kind, pair, index], recv_sem=own_r.at[kind, pair, member],
            device_id=at(mine, index, piece), device_id_type=MESH,
        )

    def to_earlier_owner(kind, pair, index):
        return pltpu.make_async_remote_copy(
            src_ref=(sk, sv)[kind].at[pair, index], dst_ref=(kl, vl)[kind].at[1, member, pair],
            send_sem=back_s.at[kind, pair, index], recv_sem=back_r.at[kind, pair, member],
            device_id=at(mine - 1, index, piece), device_id_type=MESH,
        )

    def landed(target, sem):
        pltpu.make_async_copy(target, target, sem).wait()

    order = ((0, 1), (2, 3))
    for kinds in order:
        for pair in range(pairs):
            for step in range(1, group):
                for kind in kinds:
                    spread(kind, pair, step).start()
            for kind in kinds:
                source = (k_ref, v_ref, q_ref, do_ref)[kind]
                base = (group, group, 0, 0)[kind]
                (kg, vg, qg, dg)[kind][pair, block(base + member), :] = source[:, cols(member, pair)]
            if kinds == (0, 1):

                @pl.when(has_next)
                def _(pair=pair):
                    for kind in (0, 1):
                        forward(kind, pair, member).start()

    @pl.when(jnp.logical_not(has_prev))
    def _():
        for pair in range(pairs):
            kg[pair, :band, :] = jnp.zeros((band, LANES), kg.dtype)
            vg[pair, :band, :] = jnp.zeros((band, LANES), vg.dtype)

    flips = mirror(2 * rows)
    flip = flips[rows:, :rows]
    feature = lax.broadcasted_iota(jnp.int32, (HEAD_DIM, LANES), 0)
    twice = (lax.rem(lax.broadcasted_iota(jnp.int32, (HEAD_DIM, LANES), 1), HEAD_DIM) == feature).astype(jnp.float32)
    for index in range(group):
        turned = dot(flip, emb_ref[(group - 1 - index) * rows : (group - index) * rows, :])
        ee[index * rows : (index + 1) * rows, :] = dot(
            turned.astype(jnp.bfloat16), twice.astype(jnp.bfloat16)
        ).astype(jnp.bfloat16)
    en[...] = dot(emb_ref[...], twice.astype(jnp.bfloat16)).astype(jnp.bfloat16)
    det[...] = jnp.zeros_like(det)

    for pair in range(pairs):
        for step in range(1, group):
            for kind in (0, 1):
                spread(kind, pair, step).wait_recv()

            @pl.when(has_next)
            def _(pair=pair, step=step):
                for kind in (0, 1):
                    forward(kind, pair, lax.rem(member + group - step, group)).start()

    scale = HEAD_DIM ** (-0.5)
    lane = lax.broadcasted_iota(jnp.int32, (1, LANES), 1)
    low = (lane < HEAD_DIM).astype(jnp.float32)
    high = 1.0 - low

    def halves(value, factor):
        return jnp.concatenate(
            [value * (low * factor).astype(jnp.bfloat16), value * (high * factor).astype(jnp.bfloat16)], axis=0
        )

    for pair in range(pairs):
        for step in range(1, group):
            for kind in (2, 3):
                spread(kind, pair, step).wait_recv()

        @pl.when(has_prev)
        def _(pair=pair):
            for index in range(group):
                for kind in (0, 1):
                    forward(kind, pair, index).wait_recv()

        dkt[...] = jnp.zeros_like(dkt)
        dvt[...] = jnp.zeros_like(dvt)

        def step_block(index, carry, pair=pair):
            start = pl.multiple_of(index * rows, rows)
            span = pl.ds(start, window)
            q2 = halves(qg[pair, pl.ds(start, rows), :], scale)
            do2 = halves(dg[pair, pl.ds(start, rows), :], 1.0)
            keys, vals = kg[pair, span, :], vg[pair, span, :]
            emb = ee[...]
            along = dot(q2, emb, NT)
            along = jnp.concatenate([along, jnp.full((2 * rows, rows), NEG, jnp.float32)], axis=1)
            along = jnp.concatenate([skew(along[:rows]), skew(along[rows:])], axis=0)
            column = lax.broadcasted_iota(jnp.int32, (1, window), 1) + start + jnp.where(has_prev, band, 0)
            absent = jnp.where(column < band, NEG, 0.0)
            score = dot(q2, keys, NT) + along + absent
            top = jnp.max(score, axis=1, keepdims=True)
            expd = jnp.exp(score - top)
            prob = expd * (1.0 / jnp.sum(expd, axis=1, keepdims=True))
            prob_b = prob.astype(jnp.bfloat16)
            dprob = dot(do2, vals, NT)
            delta = jnp.sum(prob_b.astype(jnp.float32) * dprob, axis=1, keepdims=True)
            dscore = prob * (dprob - delta)
            dscore_b = dscore.astype(jnp.bfloat16)
            dalong = reverse_columns(dscore_b, flips)
            dalong = jnp.concatenate([skew(dalong[:rows]), skew(dalong[rows:])], axis=0)
            dalong_b = dalong[:, rows:].astype(jnp.bfloat16)
            gq2 = dot(dscore_b, keys) + dot(dalong_b, en[...])
            gq = gq2[:rows] * (low * scale) + gq2[rows:] * (high * scale)
            sq[pair, index] = gq.astype(jnp.bfloat16)
            q2t, do2t = q2.T, do2.T
            dkt[:, span] += dot(q2t, dscore_b)
            dvt[:, span] += dot(do2t, prob_b)
            det[...] += dot(q2t, dalong_b)

            @pl.when(index != member)
            def _():
                to_query_owner(pair, index).start()

            @pl.when(has_prev)
            def _():
                sk[pair, index] = dkt[:, pl.ds(start, rows)].T.astype(jnp.bfloat16)
                sv[pair, index] = dvt[:, pl.ds(start, rows)].T.astype(jnp.bfloat16)
                for kind in (0, 1):
                    to_earlier_owner(kind, pair, index).start()

            return carry

        lax.fori_loop(0, group, step_block, 0)

        if pair == pairs - 1:
            de_own[...] = det[:HEAD_DIM, :] + det[HEAD_DIM:, :]
            for step in range(1, mates):
                share(mate, place, mates, feat, step, de_own, l1, e1_s, e1_r).start()

        def hand_over(index, carry, pair=pair):
            near = pl.ds(pl.multiple_of(band + index * rows, rows), rows)
            sk[pair, group + index] = dkt[:, near].T.astype(jnp.bfloat16)
            sv[pair, group + index] = dvt[:, near].T.astype(jnp.bfloat16)

            @pl.when(index != member)
            def _():
                for kind in (0, 1):
                    to_key_owner(kind, pair, index).start()

            return carry

        lax.fori_loop(0, group, hand_over, 0)
        ql[member, pair] = sq[pair, member]
        kl[0, member, pair] = sk[pair, group + member]
        vl[0, member, pair] = sv[pair, group + member]

    own_rows = pl.ds(pl.multiple_of(place * feat, feat), feat)
    l1[place] = de_own[own_rows, :]
    for step in range(1, mates):
        share(mate, place, mates, feat, step, de_own, l1, e1_s, e1_r).wait_recv()
    total = l1[0]
    for index in range(1, mates):
        total = total + l1[index]
    s2[...] = total
    l2[mine] = total

    def across(step):
        return pltpu.make_async_remote_copy(
            src_ref=s2, dst_ref=l2.at[mine], send_sem=e2_s.at[step], recv_sem=e2_r.at[step],
            device_id=at(lax.rem(mine + step, groups), member, piece), device_id_type=MESH,
        )

    def give(step):
        return pltpu.make_async_remote_copy(
            src_ref=s3, dst_ref=de_all.at[own_rows], send_sem=e3_s.at[step], recv_sem=e3_r.at[step],
            device_id=mate(step)[1], device_id_type=MESH,
        )

    for step in range(1, groups):
        across(step).start()

    for pair in range(pairs):
        for step in range(1, group):
            source = lax.rem(member + step, group)
            landed(ql.at[source, pair], q_r.at[pair, source])
        for index in range(group):
            gq_ref[:, (index * pairs + pair) * LANES : (index * pairs + pair + 1) * LANES] = ql[index, pair]

    for step in range(1, groups):
        across(step).wait_recv()
    total = l2[0]
    for index in range(1, groups):
        total = total + l2[index]
    s3[...] = total
    de_all[own_rows, :] = total
    for step in range(1, mates):
        give(step).start()

    for pair in range(pairs):
        for step in range(1, group):
            source = lax.rem(member + step, group)
            for kind in (0, 1):
                landed((kl, vl)[kind].at[0, source, pair], own_r.at[kind, pair, source])

        @pl.when(has_next)
        def _(pair=pair):
            for source in range(group):
                for kind in (0, 1):
                    landed((kl, vl)[kind].at[1, source, pair], back_r.at[kind, pair, source])

        @pl.when(jnp.logical_not(has_next))
        def _(pair=pair):
            for source in range(group):
                for land in (kl, vl):
                    land[1, source, pair] = jnp.zeros((rows, LANES), land.dtype)

        for index in range(group):
            spot = slice((index * pairs + pair) * LANES, (index * pairs + pair + 1) * LANES)
            for land, out in ((kl, gk_ref), (vl, gv_ref)):
                out[:, spot] = (
                    land[0, index, pair].astype(jnp.float32) + land[1, index, pair].astype(jnp.float32)
                ).astype(jnp.bfloat16)

    for step in range(1, mates):
        give(step).wait_recv()
    ge_ref[...] = de_all[...].T

    for pair in range(pairs):
        for step in range(1, group):
            for kind in range(4):
                spread(kind, pair, step).wait_send()
        for index in range(group):

            @pl.when(has_next)
            def _(pair=pair, index=index):
                for kind in (0, 1):
                    forward(kind, pair, index).wait_send()

            @pl.when(has_prev)
            def _(pair=pair, index=index):
                for kind in (0, 1):
                    to_earlier_owner(kind, pair, index).wait_send()

            @pl.when(index != member)
            def _(pair=pair, index=index):
                to_query_owner(pair, index).wait_send()
                for kind in (0, 1):
                    to_key_owner(kind, pair, index).wait_send()

    for step in range(1, mates):
        share(mate, place, mates, feat, step, de_own, l1, e1_s, e1_r).wait_send()
        give(step).wait_send()
    for step in range(1, groups):
        across(step).wait_send()


def share(mate, place, mates, feat, step, de_own, l1, e1_s, e1_r):
    other, device = mate(step)
    return pltpu.make_async_remote_copy(
        src_ref=de_own.at[pl.ds(pl.multiple_of(other * feat, feat), feat)],
        dst_ref=l1.at[place],
        send_sem=e1_s.at[step], recv_sem=e1_r.at[step],
        device_id=device, device_id_type=MESH,
    )


def grouped(seq_count, piece_count, query, key_rows, value_matrix_rows, grad_out, rel_embed):
    rows, width = query.shape
    group = BAND_EXTENT // rows
    pairs = width // (group * LANES)
    groups, mates = seq_count // group, group * piece_count
    feat = HEAD_DIM // mates
    b16, f32 = jnp.bfloat16, jnp.float32
    vmem, dma = pltpu.VMEM, pltpu.SemaphoreType.DMA
    out = jax.ShapeDtypeStruct((rows, width), b16)
    whole = pl.BlockSpec(memory_space=pltpu.VMEM)
    return pl.pallas_call(
        functools.partial(band_kernel, seq_count, piece_count, group, pairs),
        out_shape=(out, out, out, jax.ShapeDtypeStruct((BAND_EXTENT, HEAD_DIM), f32)),
        in_specs=[whole] * 5,
        out_specs=(whole,) * 4,
        scratch_shapes=[
            vmem((pairs, group * rows, LANES), b16), vmem((pairs, group * rows, LANES), b16),
            vmem((pairs, 2 * group * rows, LANES), b16), vmem((pairs, 2 * group * rows, LANES), b16),
            vmem((group, pairs, rows, LANES), b16),
            vmem((2, group, pairs, rows, LANES), b16), vmem((2, group, pairs, rows, LANES), b16),
            vmem((pairs, group, rows, LANES), b16),
            vmem((pairs, 2 * group, rows, LANES), b16), vmem((pairs, 2 * group, rows, LANES), b16),
            vmem((LANES, 2 * group * rows), f32), vmem((LANES, 2 * group * rows), f32),
            vmem((LANES, BAND_EXTENT), f32), vmem((BAND_EXTENT, LANES), b16), vmem((BAND_EXTENT, LANES), b16),
            vmem((HEAD_DIM, BAND_EXTENT), f32), vmem((mates, feat, BAND_EXTENT), f32),
            vmem((feat, BAND_EXTENT), f32), vmem((groups, feat, BAND_EXTENT), f32),
            vmem((feat, BAND_EXTENT), f32), vmem((HEAD_DIM, BAND_EXTENT), f32),
            dma((4, pairs, group)), dma((4, pairs, group)),
            dma((2, pairs, group)), dma((2, pairs, group)),
            dma((pairs, group)), dma((pairs, group)),
            dma((2, pairs, group)), dma((2, pairs, group)),
            dma((2, pairs, group)), dma((2, pairs, group)),
            dma((mates,)), dma((mates,)), dma((groups,)), dma((groups,)), dma((mates,)), dma((mates,)),
        ],
        compiler_params=pltpu.CompilerParams(
            collective_id=0, has_side_effects=True, vmem_limit_bytes=40 * 2**20
        ),
    )(query, key_rows, value_matrix_rows, grad_out, rel_embed)


def shifted(value, axis, steps):
    count = lax.axis_size(axis)
    leading, last = (max(0, -steps), min(count, count - steps))
    return lax.ppermute(value, axis, [(source, source + steps) for source in range(leading, last)])


def skew_rel(along):
    head_count, row_tiles, cols = along.shape
    padded = jnp.pad(along, ((0, 0), (0, 0), (0, row_tiles)))
    flat = padded.reshape(head_count, row_tiles * (cols + row_tiles))[
        :, : row_tiles * (cols + row_tiles - 1)
    ]
    return flat.reshape(head_count, row_tiles, cols + row_tiles - 1)[
        :, :, row_tiles : 2 * row_tiles
    ]


def unskew_rel(dscore, cols):
    zeros = jnp.zeros(dscore.shape[:2] + (cols,), dscore.dtype)
    _, pull = jax.vjp(skew_rel, zeros)
    return pull(dscore)[0]


def embed_slice(emb_pad, offset, row_tiles):
    return emb_pad[offset + 1 : offset + 2 * row_tiles + 1][::-1]


def masked_scores(query, keys, slab, offset, present, scale):
    row_tiles = query.shape[0]
    direct = jnp.einsum("thd,shd->hts", query, keys, preferred_element_type=jnp.float32)
    along = jnp.einsum("thd,rd->htr", query, slab, preferred_element_type=jnp.float32)
    score = scale * (direct + skew_rel(along))
    qpos = lax.broadcasted_iota(jnp.int32, (row_tiles, row_tiles), 0)
    kpos = lax.broadcasted_iota(jnp.int32, (row_tiles, row_tiles), 1)
    dist = offset + qpos - kpos
    valid = (dist >= 0) & (dist < BAND_EXTENT) & present
    return jnp.where(valid[None], score, -jnp.inf)


def pair_grads(prob, query, value_tensor, dout, delta, scale):
    prob_b = prob.astype(jnp.bfloat16)
    dprob = jnp.einsum("thd,shd->hts", dout, value_tensor, preferred_element_type=jnp.float32)
    dscore = (prob * (dprob - delta[:, :, None]) * scale).astype(jnp.bfloat16)
    gkey = jnp.einsum("hts,thd->shd", dscore, query, preferred_element_type=jnp.float32)
    gvalue = jnp.einsum("hts,thd->shd", prob_b, dout, preferred_element_type=jnp.float32)
    return (dscore, gkey, gvalue)


def query_terms(dscore, keys, slab, query):
    dalong = unskew_rel(dscore, slab.shape[0])
    gquery = jnp.einsum("hts,shd->thd", dscore, keys, preferred_element_type=jnp.float32)
    gquery = gquery + jnp.einsum("htr,rd->thd", dalong, slab, preferred_element_type=jnp.float32)
    gembed = jnp.einsum("htr,thd->rd", dalong, query, preferred_element_type=jnp.float32)
    return (gquery, gembed)


def local(query, key_rows, value_matrix_rows, grad_out, rel_embed):
    row_tiles = query.shape[0]
    width = query.shape[1]
    head_feature_width = HEAD_DIM
    head_count = width // head_feature_width
    scale = head_feature_width ** (-0.5)
    reach = BAND_EXTENT // row_tiles
    here = lax.axis_index("seq")
    qh = query.reshape(row_tiles, head_count, head_feature_width)
    kh = key_rows.reshape(row_tiles, head_count, head_feature_width)
    vh = value_matrix_rows.reshape(row_tiles, head_count, head_feature_width)
    doh = grad_out.reshape(row_tiles, head_count, head_feature_width)
    emb_pad = jnp.pad(rel_embed, ((row_tiles, row_tiles + 1), (0, 0)))
    slabs = [embed_slice(emb_pad, step * row_tiles, row_tiles) for step in range(reach + 1)]
    windows = [(kh, vh)]
    for step in range(1, reach + 1):
        windows.append(shifted((kh, vh), "seq", step))
    scores = [
        masked_scores(qh, windows[step][0], slabs[step], step * row_tiles, here >= step, scale)
        for step in range(reach + 1)
    ]
    top = scores[0].max(axis=2)
    for score in scores[1:]:
        top = jnp.maximum(top, score.max(axis=2))
    total = jnp.zeros_like(top)
    for score in scores:
        total = total + jnp.exp(score - top[:, :, None]).sum(axis=2)
    lse = top + jnp.log(total)
    probs = [jnp.exp(score - lse[:, :, None]) for score in scores]
    attn_out = jnp.zeros((row_tiles, head_count, head_feature_width), jnp.float32)
    for step in range(reach + 1):
        attn_out = attn_out + jnp.einsum(
            "hts,shd->thd",
            probs[step].astype(jnp.bfloat16),
            windows[step][1],
            preferred_element_type=jnp.float32,
        )
    delta = jnp.sum(doh.astype(jnp.float32) * attn_out, axis=2).T
    grad_q = jnp.zeros((row_tiles, head_count, head_feature_width), jnp.float32)
    emb_grad = jnp.zeros(emb_pad.shape, jnp.float32)
    key_parts = []
    value_parts = []
    for step in range(reach + 1):
        dscore, gkey, gvalue = pair_grads(probs[step], qh, windows[step][1], doh, delta, scale)
        gquery, gembed = query_terms(dscore, windows[step][0], slabs[step], qh)
        grad_q = grad_q + gquery
        offset = step * row_tiles
        emb_grad = emb_grad.at[offset + 1 : offset + 2 * row_tiles + 1].add(gembed[::-1])
        key_parts.append(gkey)
        value_parts.append(gvalue)
    grad_k = key_parts[0]
    grad_v = value_parts[0]
    for step in range(1, reach + 1):
        back_k, back_v = shifted((key_parts[step], value_parts[step]), "seq", -step)
        grad_k = grad_k + back_k
        grad_v = grad_v + back_v
    local_embed = emb_grad[row_tiles : row_tiles + BAND_EXTENT]
    grad_embed = lax.psum(local_embed, ("seq", "piece"))
    grad_query = grad_q.reshape(row_tiles, width).astype(jnp.bfloat16)
    grad_key = grad_k.reshape(row_tiles, width).astype(jnp.bfloat16)
    grad_value = grad_v.reshape(row_tiles, width).astype(jnp.bfloat16)
    return (grad_query, grad_key, grad_value, grad_embed)


def solution(mesh):
    placed = (P("seq", "piece"), P("seq", "piece"), P("seq", "piece"), P("seq", "piece"), P())
    seq_count, piece_count = mesh.shape["seq"], mesh.shape["piece"]

    def body(query, key_rows, value_matrix_rows, grad_out, rel_embed):
        rows, width = query.shape
        group = BAND_EXTENT // rows
        mates = group * piece_count
        if rows == LANES and seq_count % group == 0 and width % (group * LANES) == 0 and HEAD_DIM % (8 * mates) == 0:
            return grouped(seq_count, piece_count, query, key_rows, value_matrix_rows, grad_out, rel_embed)
        return local(query, key_rows, value_matrix_rows, grad_out, rel_embed)

    return jax.shard_map(
        body,
        mesh=mesh,
        in_specs=placed,
        out_specs=(P("seq", "piece"), P("seq", "piece"), P("seq", "piece"), P()),
        check_vma=False,
    )
```

```python
import functools

import jax
import jax.numpy as jnp
from jax import lax
from jax.experimental import pallas as pl
from jax.experimental.pallas import tpu as pltpu
from jax.sharding import PartitionSpec as P

HEAD_DIM = 64
BAND_EXTENT = 512
LANES = 128
MESH = pl.DeviceIdType.MESH
NT = (((1,), (1,)), ((), ()))
NEG = float("-inf")


def dot(left, right, dims=(((1,), (0,)), ((), ()))):
    return lax.dot_general(left, right, dims, preferred_element_type=jnp.float32)


def skew(along):
    return pltpu.roll(along, 1, 1, stride=1, stride_axis=0)


def mirror(size):
    down = lax.broadcasted_iota(jnp.int32, (size, size), 0)
    across = lax.broadcasted_iota(jnp.int32, (size, size), 1)
    return (down + across == size - 1).astype(jnp.float32).astype(jnp.bfloat16)


def reverse_columns(value, flips):
    parts, stop = [], value.shape[1]
    wide = flips.shape[0]
    while stop:
        size = stop % wide or wide
        parts.append(dot(value[:, stop - size : stop], flips[wide - size :, :size]))
        stop -= size
    return jnp.concatenate(parts, axis=1)


def band_kernel(
    seq_count, piece_count, group, pairs,
    q_ref, k_ref, v_ref, do_ref, emb_ref,
    gq_ref, gk_ref, gv_ref, ge_ref,
    qg, dg, kg, vg, ql, kl, vl, sq, sk, sv, dkt, dvt, det, ee, en,
    de_own, l1, s2, l2, s3, de_all,
    in_s, in_r, h_s, h_r, q_s, q_r, own_s, own_r, back_s, back_r, e1_s, e1_r, e2_s, e2_r, e3_s, e3_r,
):
    rows = q_ref.shape[0]
    band = group * rows
    window = band + rows
    groups = seq_count // group
    mates = group * piece_count
    feat = HEAD_DIM // mates
    seq, piece = lax.axis_index("seq"), lax.axis_index("piece")
    mine, member = seq // group, seq % group
    place = member * piece_count + piece
    has_prev, has_next = mine > 0, mine < groups - 1

    def at(which, index, core):
        return (which * group + index, core)

    def mate(step):
        other = lax.rem(place + step, mates)
        return other, at(mine, other // piece_count, lax.rem(other, piece_count))

    barrier = pltpu.get_barrier_semaphore()

    def greet(device):
        pl.semaphore_signal(barrier, inc=1, device_id=device, device_id_type=MESH)

    for step in range(1, mates):
        greet(mate(step)[1])
    for step in range(1, groups):
        greet(at(lax.rem(mine + step, groups), member, piece))

    @pl.when(has_prev)
    def _():
        for step in range(1, group):
            greet(at(mine - 1, lax.rem(member + step, group), piece))

    @pl.when(has_next)
    def _():
        for step in range(1, group):
            greet(at(mine + 1, lax.rem(member + step, group), piece))

    sides = jnp.where(has_prev, 1, 0) + jnp.where(has_next, 1, 0)
    pl.semaphore_wait(barrier, mates - 1 + groups - 1 + (group - 1) * sides)

    def cols(owner, pair):
        return pl.ds(pl.multiple_of((owner * pairs + pair) * LANES, LANES), LANES)

    def block(index):
        return pl.ds(pl.multiple_of(index * rows, rows), rows)

    def spread(kind, pair, step):
        source = (k_ref, v_ref, q_ref, do_ref)[kind]
        target = (kg, vg, qg, dg)[kind]
        base = (group, group, 0, 0)[kind]
        to = lax.rem(member + step, group)
        return pltpu.make_async_remote_copy(
            src_ref=source.at[:, cols(to, pair)],
            dst_ref=target.at[pair, block(base + member)],
            send_sem=in_s.at[kind, pair, step], recv_sem=in_r.at[kind, pair, step],
            device_id=at(mine, to, piece), device_id_type=MESH,
        )

    def keep(kind, pair):
        source = (k_ref, v_ref, q_ref, do_ref)[kind]
        target = (kg, vg, qg, dg)[kind]
        base = (group, group, 0, 0)[kind]
        return pltpu.make_async_copy(
            source.at[:, cols(member, pair)], target.at[pair, block(base + member)], in_s.at[kind, pair, 0]
        )

    def forward(kind, pair, index):
        target = (kg, vg)[kind]
        return pltpu.make_async_remote_copy(
            src_ref=target.at[pair, block(group + index)],
            dst_ref=target.at[pair, block(index)],
            send_sem=h_s.at[kind, pair, index], recv_sem=h_r.at[kind, pair, index],
            device_id=at(mine + 1, member, piece), device_id_type=MESH,
        )

    def to_query_owner(pair, index):
        return pltpu.make_async_remote_copy(
            src_ref=sq.at[pair, index], dst_ref=ql.at[member, pair],
            send_sem=q_s.at[pair, index], recv_sem=q_r.at[pair, member],
            device_id=at(mine, index, piece), device_id_type=MESH,
        )

    def to_key_owner(kind, pair, index):
        return pltpu.make_async_remote_copy(
            src_ref=(sk, sv)[kind].at[pair, group + index], dst_ref=(kl, vl)[kind].at[0, member, pair],
            send_sem=own_s.at[kind, pair, index], recv_sem=own_r.at[kind, pair, member],
            device_id=at(mine, index, piece), device_id_type=MESH,
        )

    def to_earlier_owner(kind, pair, index):
        return pltpu.make_async_remote_copy(
            src_ref=(sk, sv)[kind].at[pair, index], dst_ref=(kl, vl)[kind].at[1, member, pair],
            send_sem=back_s.at[kind, pair, index], recv_sem=back_r.at[kind, pair, member],
            device_id=at(mine - 1, index, piece), device_id_type=MESH,
        )

    def landed(target, sem):
        pltpu.make_async_copy(target, target, sem).wait()

    for pair in range(pairs):
        for kinds in ((0, 1), (2, 3)):
            for step in range(1, group):
                for kind in kinds:
                    spread(kind, pair, step).start()
            for kind in kinds:
                keep(kind, pair).start()
            if kinds == (0, 1):
                for kind in kinds:
                    keep(kind, pair).wait()

                @pl.when(has_next)
                def _(pair=pair):
                    for kind in (0, 1):
                        forward(kind, pair, member).start()

    @pl.when(jnp.logical_not(has_prev))
    def _():
        for pair in range(pairs):
            kg[pair, :band, :] = jnp.zeros((band, LANES), kg.dtype)
            vg[pair, :band, :] = jnp.zeros((band, LANES), vg.dtype)

    flips = mirror(2 * rows)
    flip = flips[rows:, :rows]
    feature = lax.broadcasted_iota(jnp.int32, (HEAD_DIM, LANES), 0)
    twice = (lax.rem(lax.broadcasted_iota(jnp.int32, (HEAD_DIM, LANES), 1), HEAD_DIM) == feature).astype(jnp.float32)
    for index in range(group):
        turned = dot(flip, emb_ref[(group - 1 - index) * rows : (group - index) * rows, :])
        ee[index * rows : (index + 1) * rows, :] = dot(
            turned.astype(jnp.bfloat16), twice.astype(jnp.bfloat16)
        ).astype(jnp.bfloat16)
    en[...] = dot(emb_ref[...], twice.astype(jnp.bfloat16)).astype(jnp.bfloat16)
    det[...] = jnp.zeros_like(det)

    scale = HEAD_DIM ** (-0.5)
    lane = lax.broadcasted_iota(jnp.int32, (1, LANES), 1)
    low = (lane < HEAD_DIM).astype(jnp.float32)
    high = 1.0 - low

    def halves(value, factor):
        return jnp.concatenate(
            [value * (low * factor).astype(jnp.bfloat16), value * (high * factor).astype(jnp.bfloat16)], axis=0
        )

    def pass_on(pair, step):
        for kind in (0, 1):
            spread(kind, pair, step).wait_recv()

        @pl.when(has_next)
        def _():
            for kind in (0, 1):
                forward(kind, pair, lax.rem(member + group - step, group)).start()

    for step in range(1, group):
        pass_on(0, step)

    for pair in range(pairs):
        for kind in (2, 3):
            keep(kind, pair).wait()
            for step in range(1, group):
                spread(kind, pair, step).wait_recv()

        @pl.when(has_prev)
        def _(pair=pair):
            for index in range(group):
                for kind in (0, 1):
                    forward(kind, pair, index).wait_recv()

        dkt[...] = jnp.zeros_like(dkt)
        dvt[...] = jnp.zeros_like(dvt)

        def step_block(index, carry, pair=pair):
            if pair < pairs - 1:

                @pl.when(index > 0)
                def _():
                    pass_on(pair + 1, index)

            start = pl.multiple_of(index * rows, rows)
            span = pl.ds(start, window)
            q2 = halves(qg[pair, pl.ds(start, rows), :], scale)
            do2 = halves(dg[pair, pl.ds(start, rows), :], 1.0)
            keys, vals = kg[pair, span, :], vg[pair, span, :]
            emb = ee[...]
            along = dot(q2, emb, NT)
            along = jnp.concatenate([along, jnp.full((2 * rows, rows), NEG, jnp.float32)], axis=1)
            along = jnp.concatenate([skew(along[:rows]), skew(along[rows:])], axis=0)
            column = lax.broadcasted_iota(jnp.int32, (1, window), 1) + start + jnp.where(has_prev, band, 0)
            absent = jnp.where(column < band, NEG, 0.0)
            score = dot(q2, keys, NT) + along + absent
            top = jnp.max(score, axis=1, keepdims=True)
            expd = jnp.exp(score - top)
            prob = expd * (1.0 / jnp.sum(expd, axis=1, keepdims=True))
            prob_b = prob.astype(jnp.bfloat16)
            dprob = dot(do2, vals, NT)
            delta = jnp.sum(prob_b.astype(jnp.float32) * dprob, axis=1, keepdims=True)
            dscore = prob * (dprob - delta)
            dscore_b = dscore.astype(jnp.bfloat16)
            dalong = reverse_columns(dscore_b, flips)
            dalong = jnp.concatenate([skew(dalong[:rows]), skew(dalong[rows:])], axis=0)
            dalong_b = dalong[:, rows:].astype(jnp.bfloat16)
            gq2 = dot(dscore_b, keys) + dot(dalong_b, en[...])
            gq = gq2[:rows] * (low * scale) + gq2[rows:] * (high * scale)
            sq[pair, index] = gq.astype(jnp.bfloat16)
            q2t, do2t = q2.T, do2.T
            dkt[:, span] += dot(q2t, dscore_b)
            dvt[:, span] += dot(do2t, prob_b)
            det[...] += dot(q2t, dalong_b)

            @pl.when(index != member)
            def _():
                to_query_owner(pair, index).start()

            @pl.when(has_prev)
            def _():
                sk[pair, index] = dkt[:, pl.ds(start, rows)].T.astype(jnp.bfloat16)
                sv[pair, index] = dvt[:, pl.ds(start, rows)].T.astype(jnp.bfloat16)
                for kind in (0, 1):
                    to_earlier_owner(kind, pair, index).start()

            return carry

        lax.fori_loop(0, group, step_block, 0)

        if pair == pairs - 1:
            de_own[...] = det[:HEAD_DIM, :] + det[HEAD_DIM:, :]
            for step in range(1, mates):
                share(mate, place, mates, feat, step, de_own, l1, e1_s, e1_r).start()

        def hand_over(index, carry, pair=pair):
            near = pl.ds(pl.multiple_of(band + index * rows, rows), rows)
            sk[pair, group + index] = dkt[:, near].T.astype(jnp.bfloat16)
            sv[pair, group + index] = dvt[:, near].T.astype(jnp.bfloat16)

            @pl.when(index != member)
            def _():
                for kind in (0, 1):
                    to_key_owner(kind, pair, index).start()

            return carry

        lax.fori_loop(0, group, hand_over, 0)
        ql[member, pair] = sq[pair, member]
        kl[0, member, pair] = sk[pair, group + member]
        vl[0, member, pair] = sv[pair, group + member]

    own_rows = pl.ds(pl.multiple_of(place * feat, feat), feat)
    l1[place] = de_own[own_rows, :]
    for step in range(1, mates):
        share(mate, place, mates, feat, step, de_own, l1, e1_s, e1_r).wait_recv()
    total = l1[0]
    for index in range(1, mates):
        total = total + l1[index]
    s2[...] = total
    l2[mine] = total

    def across(step):
        return pltpu.make_async_remote_copy(
            src_ref=s2, dst_ref=l2.at[mine], send_sem=e2_s.at[step], recv_sem=e2_r.at[step],
            device_id=at(lax.rem(mine + step, groups), member, piece), device_id_type=MESH,
        )

    def give(step):
        return pltpu.make_async_remote_copy(
            src_ref=s3, dst_ref=de_all.at[own_rows], send_sem=e3_s.at[step], recv_sem=e3_r.at[step],
            device_id=mate(step)[1], device_id_type=MESH,
        )

    for step in range(1, groups):
        across(step).start()

    for step in range(1, groups):
        across(step).wait_recv()
    total = l2[0]
    for index in range(1, groups):
        total = total + l2[index]
    s3[...] = total
    de_all[own_rows, :] = total
    for step in range(1, mates):
        give(step).start()

    for pair in range(pairs):
        for step in range(1, group):
            source = lax.rem(member + step, group)
            landed(ql.at[source, pair], q_r.at[pair, source])
        for index in range(group):
            gq_ref[:, (index * pairs + pair) * LANES : (index * pairs + pair + 1) * LANES] = ql[index, pair]

    for pair in range(pairs):
        for step in range(1, group):
            source = lax.rem(member + step, group)
            for kind in (0, 1):
                landed((kl, vl)[kind].at[0, source, pair], own_r.at[kind, pair, source])

        @pl.when(has_next)
        def _(pair=pair):
            for source in range(group):
                for kind in (0, 1):
                    landed((kl, vl)[kind].at[1, source, pair], back_r.at[kind, pair, source])

        @pl.when(jnp.logical_not(has_next))
        def _(pair=pair):
            for source in range(group):
                for land in (kl, vl):
                    land[1, source, pair] = jnp.zeros((rows, LANES), land.dtype)

        for index in range(group):
            spot = slice((index * pairs + pair) * LANES, (index * pairs + pair + 1) * LANES)
            for land, out in ((kl, gk_ref), (vl, gv_ref)):
                out[:, spot] = (
                    land[0, index, pair].astype(jnp.float32) + land[1, index, pair].astype(jnp.float32)
                ).astype(jnp.bfloat16)

    for step in range(1, mates):
        give(step).wait_recv()
    ge_ref[...] = de_all[...].T

    for pair in range(pairs):
        for step in range(1, group):
            for kind in range(4):
                spread(kind, pair, step).wait_send()
        for index in range(group):

            @pl.when(has_next)
            def _(pair=pair, index=index):
                for kind in (0, 1):
                    forward(kind, pair, index).wait_send()

            @pl.when(has_prev)
            def _(pair=pair, index=index):
                for kind in (0, 1):
                    to_earlier_owner(kind, pair, index).wait_send()

            @pl.when(index != member)
            def _(pair=pair, index=index):
                to_query_owner(pair, index).wait_send()
                for kind in (0, 1):
                    to_key_owner(kind, pair, index).wait_send()

    for step in range(1, mates):
        share(mate, place, mates, feat, step, de_own, l1, e1_s, e1_r).wait_send()
        give(step).wait_send()
    for step in range(1, groups):
        across(step).wait_send()


def share(mate, place, mates, feat, step, de_own, l1, e1_s, e1_r):
    other, device = mate(step)
    return pltpu.make_async_remote_copy(
        src_ref=de_own.at[pl.ds(pl.multiple_of(other * feat, feat), feat)],
        dst_ref=l1.at[place],
        send_sem=e1_s.at[step], recv_sem=e1_r.at[step],
        device_id=device, device_id_type=MESH,
    )


def grouped(seq_count, piece_count, query, key_rows, value_matrix_rows, grad_out, rel_embed):
    rows, width = query.shape
    group = BAND_EXTENT // rows
    pairs = width // (group * LANES)
    groups, mates = seq_count // group, group * piece_count
    feat = HEAD_DIM // mates
    b16, f32 = jnp.bfloat16, jnp.float32
    vmem, dma = pltpu.VMEM, pltpu.SemaphoreType.DMA
    out = jax.ShapeDtypeStruct((rows, width), b16)
    whole = pl.BlockSpec(memory_space=pltpu.VMEM)
    return pl.pallas_call(
        functools.partial(band_kernel, seq_count, piece_count, group, pairs),
        out_shape=(out, out, out, jax.ShapeDtypeStruct((BAND_EXTENT, HEAD_DIM), f32)),
        in_specs=[pl.BlockSpec(memory_space=pltpu.HBM)] * 4 + [whole],
        out_specs=(whole,) * 4,
        scratch_shapes=[
            vmem((pairs, group * rows, LANES), b16), vmem((pairs, group * rows, LANES), b16),
            vmem((pairs, 2 * group * rows, LANES), b16), vmem((pairs, 2 * group * rows, LANES), b16),
            vmem((group, pairs, rows, LANES), b16),
            vmem((2, group, pairs, rows, LANES), b16), vmem((2, group, pairs, rows, LANES), b16),
            vmem((pairs, group, rows, LANES), b16),
            vmem((pairs, 2 * group, rows, LANES), b16), vmem((pairs, 2 * group, rows, LANES), b16),
            vmem((LANES, 2 * group * rows), f32), vmem((LANES, 2 * group * rows), f32),
            vmem((LANES, BAND_EXTENT), f32), vmem((BAND_EXTENT, LANES), b16), vmem((BAND_EXTENT, LANES), b16),
            vmem((HEAD_DIM, BAND_EXTENT), f32), vmem((mates, feat, BAND_EXTENT), f32),
            vmem((feat, BAND_EXTENT), f32), vmem((groups, feat, BAND_EXTENT), f32),
            vmem((feat, BAND_EXTENT), f32), vmem((HEAD_DIM, BAND_EXTENT), f32),
            dma((4, pairs, group)), dma((4, pairs, group)),
            dma((2, pairs, group)), dma((2, pairs, group)),
            dma((pairs, group)), dma((pairs, group)),
            dma((2, pairs, group)), dma((2, pairs, group)),
            dma((2, pairs, group)), dma((2, pairs, group)),
            dma((mates,)), dma((mates,)), dma((groups,)), dma((groups,)), dma((mates,)), dma((mates,)),
        ],
        compiler_params=pltpu.CompilerParams(
            collective_id=0, has_side_effects=True, vmem_limit_bytes=40 * 2**20
        ),
    )(query, key_rows, value_matrix_rows, grad_out, rel_embed)


def shifted(value, axis, steps):
    count = lax.axis_size(axis)
    leading, last = (max(0, -steps), min(count, count - steps))
    return lax.ppermute(value, axis, [(source, source + steps) for source in range(leading, last)])


def skew_rel(along):
    head_count, row_tiles, cols = along.shape
    padded = jnp.pad(along, ((0, 0), (0, 0), (0, row_tiles)))
    flat = padded.reshape(head_count, row_tiles * (cols + row_tiles))[
        :, : row_tiles * (cols + row_tiles - 1)
    ]
    return flat.reshape(head_count, row_tiles, cols + row_tiles - 1)[
        :, :, row_tiles : 2 * row_tiles
    ]


def unskew_rel(dscore, cols):
    zeros = jnp.zeros(dscore.shape[:2] + (cols,), dscore.dtype)
    _, pull = jax.vjp(skew_rel, zeros)
    return pull(dscore)[0]


def embed_slice(emb_pad, offset, row_tiles):
    return emb_pad[offset + 1 : offset + 2 * row_tiles + 1][::-1]


def masked_scores(query, keys, slab, offset, present, scale):
    row_tiles = query.shape[0]
    direct = jnp.einsum("thd,shd->hts", query, keys, preferred_element_type=jnp.float32)
    along = jnp.einsum("thd,rd->htr", query, slab, preferred_element_type=jnp.float32)
    score = scale * (direct + skew_rel(along))
    qpos = lax.broadcasted_iota(jnp.int32, (row_tiles, row_tiles), 0)
    kpos = lax.broadcasted_iota(jnp.int32, (row_tiles, row_tiles), 1)
    dist = offset + qpos - kpos
    valid = (dist >= 0) & (dist < BAND_EXTENT) & present
    return jnp.where(valid[None], score, -jnp.inf)


def pair_grads(prob, query, value_tensor, dout, delta, scale):
    prob_b = prob.astype(jnp.bfloat16)
    dprob = jnp.einsum("thd,shd->hts", dout, value_tensor, preferred_element_type=jnp.float32)
    dscore = (prob * (dprob - delta[:, :, None]) * scale).astype(jnp.bfloat16)
    gkey = jnp.einsum("hts,thd->shd", dscore, query, preferred_element_type=jnp.float32)
    gvalue = jnp.einsum("hts,thd->shd", prob_b, dout, preferred_element_type=jnp.float32)
    return (dscore, gkey, gvalue)


def query_terms(dscore, keys, slab, query):
    dalong = unskew_rel(dscore, slab.shape[0])
    gquery = jnp.einsum("hts,shd->thd", dscore, keys, preferred_element_type=jnp.float32)
    gquery = gquery + jnp.einsum("htr,rd->thd", dalong, slab, preferred_element_type=jnp.float32)
    gembed = jnp.einsum("htr,thd->rd", dalong, query, preferred_element_type=jnp.float32)
    return (gquery, gembed)


def local(query, key_rows, value_matrix_rows, grad_out, rel_embed):
    row_tiles = query.shape[0]
    width = query.shape[1]
    head_feature_width = HEAD_DIM
    head_count = width // head_feature_width
    scale = head_feature_width ** (-0.5)
    reach = BAND_EXTENT // row_tiles
    here = lax.axis_index("seq")
    qh = query.reshape(row_tiles, head_count, head_feature_width)
    kh = key_rows.reshape(row_tiles, head_count, head_feature_width)
    vh = value_matrix_rows.reshape(row_tiles, head_count, head_feature_width)
    doh = grad_out.reshape(row_tiles, head_count, head_feature_width)
    emb_pad = jnp.pad(rel_embed, ((row_tiles, row_tiles + 1), (0, 0)))
    slabs = [embed_slice(emb_pad, step * row_tiles, row_tiles) for step in range(reach + 1)]
    windows = [(kh, vh)]
    for step in range(1, reach + 1):
        windows.append(shifted((kh, vh), "seq", step))
    scores = [
        masked_scores(qh, windows[step][0], slabs[step], step * row_tiles, here >= step, scale)
        for step in range(reach + 1)
    ]
    top = scores[0].max(axis=2)
    for score in scores[1:]:
        top = jnp.maximum(top, score.max(axis=2))
    total = jnp.zeros_like(top)
    for score in scores:
        total = total + jnp.exp(score - top[:, :, None]).sum(axis=2)
    lse = top + jnp.log(total)
    probs = [jnp.exp(score - lse[:, :, None]) for score in scores]
    attn_out = jnp.zeros((row_tiles, head_count, head_feature_width), jnp.float32)
    for step in range(reach + 1):
        attn_out = attn_out + jnp.einsum(
            "hts,shd->thd",
            probs[step].astype(jnp.bfloat16),
            windows[step][1],
            preferred_element_type=jnp.float32,
        )
    delta = jnp.sum(doh.astype(jnp.float32) * attn_out, axis=2).T
    grad_q = jnp.zeros((row_tiles, head_count, head_feature_width), jnp.float32)
    emb_grad = jnp.zeros(emb_pad.shape, jnp.float32)
    key_parts = []
    value_parts = []
    for step in range(reach + 1):
        dscore, gkey, gvalue = pair_grads(probs[step], qh, windows[step][1], doh, delta, scale)
        gquery, gembed = query_terms(dscore, windows[step][0], slabs[step], qh)
        grad_q = grad_q + gquery
        offset = step * row_tiles
        emb_grad = emb_grad.at[offset + 1 : offset + 2 * row_tiles + 1].add(gembed[::-1])
        key_parts.append(gkey)
        value_parts.append(gvalue)
    grad_k = key_parts[0]
    grad_v = value_parts[0]
    for step in range(1, reach + 1):
        back_k, back_v = shifted((key_parts[step], value_parts[step]), "seq", -step)
        grad_k = grad_k + back_k
        grad_v = grad_v + back_v
    local_embed = emb_grad[row_tiles : row_tiles + BAND_EXTENT]
    grad_embed = lax.psum(local_embed, ("seq", "piece"))
    grad_query = grad_q.reshape(row_tiles, width).astype(jnp.bfloat16)
    grad_key = grad_k.reshape(row_tiles, width).astype(jnp.bfloat16)
    grad_value = grad_v.reshape(row_tiles, width).astype(jnp.bfloat16)
    return (grad_query, grad_key, grad_value, grad_embed)


def solution(mesh):
    placed = (P("seq", "piece"), P("seq", "piece"), P("seq", "piece"), P("seq", "piece"), P())
    seq_count, piece_count = mesh.shape["seq"], mesh.shape["piece"]

    def body(query, key_rows, value_matrix_rows, grad_out, rel_embed):
        rows, width = query.shape
        group = BAND_EXTENT // rows
        mates = group * piece_count
        if rows == LANES and seq_count % group == 0 and width % (group * LANES) == 0 and HEAD_DIM % (8 * mates) == 0:
            return grouped(seq_count, piece_count, query, key_rows, value_matrix_rows, grad_out, rel_embed)
        return local(query, key_rows, value_matrix_rows, grad_out, rel_embed)

    return jax.shard_map(
        body,
        mesh=mesh,
        in_specs=placed,
        out_specs=(P("seq", "piece"), P("seq", "piece"), P("seq", "piece"), P()),
        check_vma=False,
    )
```
